512 devices in a mesh: grp: 4 (over y), resp: 16 (over z_lo, core), tp: 8 (over z_hi, x).
Axes of the slice: x: 4, y: 4, z: 16 (z_hi: 2, z_lo: 8; z = z_hi * 8 + z_lo), core: 2. Of those that a mesh axis runs over, the one named last changes fastest.
Arguments:
- queries: bfloat16 [8192, 64, 576], P(('grp', 'resp'), 'tp'), parts along dimension 0, may hold values from -44 to 44
- grad_out: bfloat16 [8192, 64, 512], P(('grp', 'resp'), 'tp'), parts along dimension 0, may hold values from -32 to 32
- prompt_kv: bfloat16 [3072, 576], P(('grp', 'resp')), parts along dimension 0, may hold values from -5 to 5
- resp_kv: bfloat16 [8192, 576], P(('grp', 'resp')), parts along dimension 0, may hold values from -6 to 6
- lengths: int32 [64], P(('grp', 'resp')), parts along dimension 0, may hold values from 16 to 128, as said below
Outputs:
- grad_queries: bfloat16 [8192, 64, 576], P(('grp', 'resp'), 'tp'), parts along dimension 0
- grad_prompt: bfloat16 [3072, 576], P(('grp', 'resp')), parts along dimension 0
- grad_resp: bfloat16 [8192, 576], P(('grp', 'resp')), parts along dimension 0
The draws below stay inside these ranges and needn't reach their ends.
There are 4 independent parts, one for each index of `grp`. The reference program is written for one: setup_inputs(seed, part) draws one part's arguments, and reference() takes and returns one part's arrays. A program takes and returns all parts, laid end to end along the dimension named above; each array names one. Nothing has to cross between parts.
Inputs may be any that keep to these rules, and one draw needn't show every extreme that they name: `lengths`: every response has length 16 or more, and some response has length 128.
All inputs are finite; a program needn't handle non-finite values.
Results may differ from the reference program's by a relative error of at most 0.012.
Values may be sent and summed in bfloat16 or wider, within the bound.
No kernel may reach another device: no remote copies, remote signals or barrier semaphores. Data moves between devices by JAX's collectives and lax.ppermute only.
A program may use at most 64 MiB of HBM per device.

```python
import jax
import jax.numpy as jnp
from jax import lax

LAT = 512
ROPE = 64
RESP_TOK = 128
HEADS = 64
PROMPT = 768
RESP_ALL = 2048
N_RESP = 16


def shared_prompt(key):
    width = LAT + ROPE
    base = jnp.clip(jax.random.normal(key, (PROMPT, width), jnp.float32), -4.0, 4.0)
    halves = base.reshape(PROMPT // 2, 2, width)
    even = halves[:, 0, :]
    odd = halves[:, 1, :]
    return jnp.stack([even, odd], 1).reshape(PROMPT, width)


def draw_prompt_kv(key, part):
    return shared_prompt(key).astype(jnp.bfloat16)


def draw_queries(key, part):
    width = LAT + ROPE
    key = jax.random.fold_in(key, 5)
    entries = jnp.clip(jax.random.normal(key, (RESP_ALL, HEADS, width), jnp.float32), -4.0, 4.0)
    return entries.astype(jnp.bfloat16)


def draw_lengths(key, part):
    key = jax.random.fold_in(key, 7)
    lower = max(1, RESP_TOK // 8)
    drawn = jax.random.randint(key, (N_RESP,), lower, RESP_TOK + 1, dtype=jnp.int32)
    pick = jax.random.randint(jax.random.fold_in(key, 1), (), 0, N_RESP, dtype=jnp.int32)
    return jnp.where(jnp.arange(N_RESP, dtype=jnp.int32) == pick, RESP_TOK, drawn).astype(jnp.int32)


def levels(stream_key, extent, cuts, least, largest):
    level, own = 1.0, jax.random.fold_in(stream_key, 6)
    for axis_at, shards_of in cuts:
        draws = jnp.exp(jax.random.uniform(jax.random.fold_in(own, axis_at), (shards_of,), jnp.float32, least / len(cuts), largest / len(cuts)))
        level = level * jnp.repeat(draws, extent[axis_at] // shards_of).reshape([-1 if axis == axis_at else 1 for axis in range(len(extent))])
    return level


def centred(stream_key, shape, deviation, reach, cuts=(), held_as=jnp.bfloat16):
    values = jax.random.normal(stream_key, shape, jnp.float32) * deviation
    if len(cuts) > 0:
        values = levels(stream_key, shape, cuts, -0.22, 0.18) * values
    return jnp.clip(values, min=-reach, max=reach).astype(held_as)


def setup_inputs(seed: int = 0, part: int = 0) -> dict:
    seeds = jax.random.split(jax.random.key(seed), 6)
    own_keys = jax.random.split(jax.random.fold_in(seeds[5], part), 6)
    return {
        "queries": draw_queries(jax.random.fold_in(jax.random.fold_in(seeds[5], part), 71), part),
        "grad_out": centred(own_keys[1], (RESP_ALL, HEADS, LAT), 6.0, 32.0, ((0, 16), (1, 8))),
        "prompt_kv": draw_prompt_kv(jax.random.fold_in(jax.random.fold_in(seeds[5], part), 71), part),
        "resp_kv": centred(own_keys[3], (RESP_ALL, LAT + ROPE), 1.0, 6.0, ((0, 16),)),
        "lengths": draw_lengths(jax.random.fold_in(jax.random.fold_in(seeds[5], part), 71), part),
    }


softmax_scale = 192 ** -0.5
masked_value = -1e30


def response_grads(queries, grad_out, prompt_kv, resp_kv, length):
    rows, heads, width = queries.shape
    latent = grad_out.shape[2]
    prompt_rows = prompt_kv.shape[0]
    keys = jnp.concatenate([prompt_kv, resp_kv], 0)
    total = keys.shape[0]
    position = jnp.arange(rows, dtype=jnp.int32)
    key_pos = jnp.arange(total, dtype=jnp.int32) - prompt_rows
    allowed = key_pos[None, :] <= position[:, None]
    live = position < length
    q_flat = queries.reshape(rows * heads, width)
    scores = jnp.dot(q_flat, keys.T, preferred_element_type=jnp.float32).reshape(rows, heads, total) * softmax_scale
    scores = jnp.where(allowed[:, None, :], scores, masked_value)
    top = jnp.max(scores, axis=-1, keepdims=True)
    expo = jnp.exp(scores - top)
    probs = (expo / jnp.sum(expo, axis=-1, keepdims=True)).reshape(rows * heads, total)
    probs_b = probs.astype(jnp.bfloat16)
    d_flat = jnp.where(live[:, None, None], grad_out, jnp.zeros_like(grad_out)).reshape(rows * heads, latent)
    values = keys[:, :latent]
    out_vals = jnp.dot(probs_b, values, preferred_element_type=jnp.float32)
    delta = jnp.sum(d_flat.astype(jnp.float32) * out_vals, axis=-1, keepdims=True)
    d_prob = jnp.dot(d_flat, values.T, preferred_element_type=jnp.float32)
    d_score = (softmax_scale * probs * (d_prob - delta)).astype(jnp.bfloat16)
    d_query = jnp.dot(d_score, keys, preferred_element_type=jnp.float32).astype(jnp.bfloat16).reshape(rows, heads, width)
    dims = (((0,), (0,)), ((), ()))
    d_keys = lax.dot_general(d_score, q_flat, dims, preferred_element_type=jnp.float32)
    d_vals = lax.dot_general(probs_b, d_flat, dims, preferred_element_type=jnp.float32)
    d_kv = jnp.concatenate([d_keys[:, :latent] + d_vals, d_keys[:, latent:]], 1)
    return d_query, d_kv[:prompt_rows], d_kv[prompt_rows:]


def reference(queries, grad_out, prompt_kv, resp_kv, lengths):
    width = LAT + ROPE
    q_all = queries.reshape(N_RESP, RESP_TOK, HEADS, width)
    d_all = grad_out.reshape(N_RESP, RESP_TOK, HEADS, LAT)
    r_all = resp_kv.reshape(N_RESP, RESP_TOK, width)

    def step(carry, item):
        q_one, d_one, r_one, length = item
        d_query, d_prompt, d_resp = response_grads(q_one, d_one, prompt_kv, r_one, length)
        return carry + d_prompt, (d_query, d_resp)

    start = jnp.zeros((PROMPT, width), jnp.float32)
    summed, (d_queries, d_resps) = lax.scan(step, start, (q_all, d_all, r_all, lengths))
    return (d_queries.reshape(RESP_ALL, HEADS, width), summed.astype(jnp.bfloat16),
            d_resps.reshape(RESP_ALL, width).astype(jnp.bfloat16))
```

```python
import functools

import jax
import jax.numpy as jnp
from jax import lax
from jax.experimental import pallas as pl
from jax.experimental.pallas import tpu as pltpu
from jax.sharding import Mesh, PartitionSpec as P

softmax_scale = 192 ** (-0.5)
log2_e = 1.4426950408889634
masked_value = -1e30
f32, bf16 = jnp.float32, jnp.bfloat16

LAT, ROPE, WIDTH = 512, 64, 576
BLOCK, PACKED = 48, 56
RESP, RESP_PACKED = 128, 144
GRID = (4, 8, 2, 2, 4)
AXES = ("grp", "zlo", "core", "zhi", "x")

SMEM = pl.BlockSpec(memory_space=pltpu.SMEM)
VMEM = pl.BlockSpec(memory_space=pltpu.VMEM)


def call(kernel, ins, out, scratch=(), limit=16, flops=0):
    moved = sum(o.size * o.dtype.itemsize for o in out)
    many = len(out) > 1
    return pl.pallas_call(
        kernel,
        out_shape=tuple(out) if many else out[0],
        in_specs=ins,
        out_specs=tuple(VMEM for _ in out) if many else VMEM,
        scratch_shapes=list(scratch),
        compiler_params=pltpu.CompilerParams(vmem_limit_bytes=limit * 2**20),
        cost_estimate=pl.CostEstimate(flops=flops, bytes_accessed=2 * moved, transcendentals=0),
    )


def shape(dims, dtype):
    return jax.ShapeDtypeStruct(dims, dtype)


def pack_prompt(x_ref, rows_ref, out_ref):
    x = x_ref[0]
    rows = rows_ref[...].astype(f32)
    lat = rows[:, 0:128]
    rope = rows[0:16, LAT:WIDTH]
    for q in range(1, 4):
        lat = jnp.where(x == q, rows[:, 128 * q : 128 * q + 128], lat)
        if q < 3:
            rope = jnp.where(x == q, rows[16 * q : 16 * q + 16, LAT:WIDTH], rope)
    rope = jnp.concatenate([rope[0:8], rope[8:16]], 1)
    block = jnp.concatenate([lat, rope], 0).astype(bf16)
    for z in range(out_ref.shape[0]):
        out_ref[z] = block


def pack_block(lat, rope, q):
    lat = lat[:, 128 * q : 128 * q + 128].reshape(8, BLOCK, 128)
    if q < 3:
        rope = rope.reshape(8, BLOCK, ROPE)[:, 16 * q : 16 * q + 16]
        rope = jnp.concatenate([rope[:, 0:8], rope[:, 8:16]], 2)
    else:
        rope = jnp.zeros((8, 8, 128), f32)
    return jnp.concatenate([lat, rope], 1)


NT = (((1,), (1,)), ((), ()))


def main_kernel(core_ref, len_ref, prompt_ref, resp_ref, q_ref, d_ref, k_ref, ds_ref, send_ref, keep_ref,
                keep_resp_ref, p_ref):
    core = core_ref[0]
    length = len_ref[0]
    for half in range(2):
        who = core if half == 0 else 1 - core
        at = 384 * half
        rope = []
        for q in range(4):
            got = prompt_ref[who, q]
            k_ref[at : at + 384, 128 * q : 128 * q + 128] = got[:, 0:48].reshape(384, 128)
            if q < 3:
                two = got[:, 48:56].astype(f32)
                rope += [two[:, :, 0:64], two[:, :, 64:128]]
        k_ref[at : at + 384, LAT:WIDTH] = jnp.concatenate(rope, 1).reshape(384, ROPE).astype(bf16)
    k_ref[768:896, :] = resp_ref[...]

    key_at = lax.broadcasted_iota(jnp.int32, (RESP, 256), 0)
    slot = lax.broadcasted_iota(jnp.int32, (RESP, 256), 1) % 128
    allowed = key_at <= slot
    live = lax.broadcasted_iota(jnp.int32, (1, 256), 1) % 128 < length
    for pair in range(4):
        q_pair = jnp.concatenate([q_ref[2 * pair], q_ref[2 * pair + 1]], 1)
        scores = jnp.dot(k_ref[...], q_pair, preferred_element_type=f32) * (softmax_scale * log2_e)
        scores = jnp.concatenate([scores[0:768], jnp.where(allowed, scores[768:896], masked_value)], 0)
        top = jnp.max(scores, axis=0, keepdims=True)
        expo = jnp.exp2(scores - top)
        total = jnp.sum(expo, axis=0, keepdims=True)
        d_pair = d_ref[256 * pair : 256 * pair + 256]
        d_prob = lax.dot_general(k_ref[:, 0:LAT], d_pair, NT, preferred_element_type=f32)
        inverse = 1.0 / total
        delta = jnp.sum(expo * d_prob, axis=0, keepdims=True) * inverse
        probs = expo * jnp.where(live, inverse, 0.0)
        p_ref[:, 256 * pair : 256 * pair + 256] = probs.astype(bf16)
        ds_ref[:, 256 * pair : 256 * pair + 256] = (probs * (d_prob - delta) * softmax_scale).astype(bf16)

    def grads(lo, hi):
        d_lat = jnp.zeros((hi - lo, LAT), f32)
        d_rope = jnp.zeros((hi - lo, ROPE), f32)
        d_lat = jnp.dot(p_ref[lo:hi], d_ref[...], preferred_element_type=f32)
        q_all = jnp.concatenate([q_ref[h] for h in range(8)], 1)
        d_lat = d_lat + lax.dot_general(ds_ref[lo:hi], q_all[0:LAT], NT, preferred_element_type=f32)
        d_rope = lax.dot_general(ds_ref[lo:hi], q_all[LAT:WIDTH], NT, preferred_element_type=f32)
        return d_lat, d_rope

    lat, rope = grads(384, 768)
    for q in range(4):
        send_ref[q] = pack_block(lat, rope, q).astype(bf16)
    lat, rope = grads(0, 384)
    for q in range(4):
        keep_ref[q] = pack_block(lat, rope, q)
    lat, rope = grads(768, 896)
    for q in range(4):
        two = rope[32 * q : 32 * q + 32]
        two = jnp.concatenate([two[0:16], two[16:32]], 1)
        keep_resp_ref[q] = jnp.concatenate([lat[:, 128 * q : 128 * q + 128], two], 0).astype(bf16)


def query_kernel(k_ref, ds_ref, out_ref):
    k_t = k_ref[...].T
    for pair in range(4):
        got = jnp.dot(k_t, ds_ref[:, 256 * pair : 256 * pair + 256], preferred_element_type=f32).astype(bf16)
        out_ref[2 * pair] = got[:, 0:128]
        out_ref[2 * pair + 1] = got[:, 128:256]


def core_sum(core_ref, got_ref, keep_ref, keep_resp_ref, out_ref):
    other = 1 - core_ref[0]
    for q in range(4):
        both = keep_ref[q] + got_ref[other, q].astype(f32)
        out_ref[q, 0:448] = both.reshape(448, 128).astype(bf16)
        out_ref[q, 448:592] = keep_resp_ref[q]


def x_sum(got_ref, prompt_ref, resp_ref):
    total = got_ref[0].astype(f32)
    for q in range(1, 4):
        total = total + got_ref[q].astype(f32)
    total = total.astype(bf16)
    for z in range(8):
        block = total[PACKED * z : PACKED * z + PACKED]
        prompt_ref[2 * z] = block
        prompt_ref[2 * z + 1] = block
    resp_ref[...] = total[448:592]


def last_sum(got_ref, mine_ref, far_ref, out_ref):
    total = got_ref[0].astype(f32)
    for z in range(1, 16):
        total = total + got_ref[z].astype(f32)
    resp = (mine_ref[...].astype(f32) + far_ref[...].astype(f32)).astype(bf16)
    total = total.astype(bf16)
    for q in range(4):
        out_ref[q, 0:RESP_PACKED] = resp
        out_ref[q, RESP_PACKED : RESP_PACKED + PACKED] = total


def unpack(got_ref, prompt_ref, resp_ref):
    resp_rope, prompt_rope = [], []
    for q in range(4):
        got = got_ref[q].astype(f32)
        resp_ref[128 * q : 128 * q + 128, :] = got[0:128].T.astype(bf16)
        resp_rope += [got[128:144, 0:64], got[128:144, 64:128]]
        prompt_ref[:, 128 * q : 128 * q + 128] = got[144:192].astype(bf16)
        if q < 3:
            prompt_rope += [got[192:200, 0:64], got[192:200, 64:128]]
    resp_ref[LAT:WIDTH, :] = jnp.concatenate(resp_rope, 0).T.astype(bf16)
    prompt_ref[:, LAT:WIDTH] = jnp.concatenate(prompt_rope, 0).astype(bf16)


def body(queries, grad_out, prompt_kv, resp_kv, lengths):
    x_at = lax.axis_index("x").astype(jnp.int32).reshape(1)
    core_at = lax.axis_index("core").astype(jnp.int32).reshape(1)
    q_t = jnp.transpose(queries, (1, 2, 0))
    d_heads = jnp.transpose(grad_out, (1, 0, 2)).reshape(8 * RESP, LAT)

    mine = call(pack_prompt, [SMEM, VMEM], [shape((8, PACKED, 128), bf16)])(x_at, prompt_kv)
    along_z = lax.all_to_all(mine, "zlo", 0, 0, tiled=True)
    along_x = lax.all_gather(along_z, "x")
    prompt = lax.all_gather(along_x, "core")

    keys, d_score, send, keep, keep_resp = call(
        main_kernel,
        [SMEM, SMEM, VMEM, VMEM, VMEM, VMEM],
        [
            shape((896, WIDTH), bf16),
            shape((896, 1024), bf16),
            shape((4, 8, PACKED, 128), bf16),
            shape((4, 8, PACKED, 128), f32),
            shape((4, RESP_PACKED, 128), bf16),
        ],
        scratch=[pltpu.VMEM((896, 1024), bf16)],
        limit=40,
        flops=4 * 2 * 1024 * 896 * 576,
    )(core_at, lengths, prompt, resp_kv, q_t, d_heads)

    got = lax.all_gather(send, "core")
    parts = call(core_sum, [SMEM, VMEM, VMEM, VMEM], [shape((4, 592, 128), bf16)])(core_at, got, keep, keep_resp)
    parts = lax.all_to_all(parts, "x", 0, 0, tiled=True)
    d_query = call(
        query_kernel, [VMEM, VMEM], [shape((8, WIDTH, 128), bf16)], limit=24, flops=2 * 1024 * 896 * 576
    )(keys, d_score)
    terms, resp_mine = call(x_sum, [VMEM], [shape((16, PACKED, 128), bf16), shape((RESP_PACKED, 128), bf16)])(parts)
    terms = lax.all_to_all(terms, ("zlo", "zhi"), 0, 0, tiled=True)
    resp_far = lax.ppermute(resp_mine, "zhi", [(0, 1), (1, 0)])
    final = call(last_sum, [VMEM, VMEM, VMEM], [shape((4, 200, 128), bf16)])(terms, resp_mine, resp_far)
    final = lax.all_to_all(final, "x", 0, 0, tiled=True)
    grad_prompt, grad_resp = call(unpack, [VMEM], [shape((BLOCK, WIDTH), bf16), shape((WIDTH, RESP), bf16)])(final)
    return (jnp.transpose(d_query, (2, 0, 1)), grad_prompt, grad_resp.T)


def solution(mesh):
    split = Mesh(mesh.devices.reshape(GRID), AXES)
    rows = ("grp", "zlo", "core")
    heads = ("zhi", "x")
    return jax.shard_map(
        body,
        mesh=split,
        in_specs=(P(rows, heads, None), P(rows, heads, None), P(rows, None), P(rows, None), P(rows)),
        out_specs=(P(rows, heads, None), P(rows, None), P(rows, None)),
        check_vma=False,
    )
```

```python
import functools

import jax
import jax.numpy as jnp
from jax import lax
from jax.experimental import pallas as pl
from jax.experimental.pallas import tpu as pltpu
from jax.sharding import Mesh, PartitionSpec as P

softmax_scale = 192 ** (-0.5)
log2_e = 1.4426950408889634
masked_value = -1e30
f32, bf16 = jnp.float32, jnp.bfloat16

LAT, ROPE, WIDTH = 512, 64, 576
BLOCK, PACKED = 48, 56
RESP, RESP_PACKED = 128, 144
GRID = (4, 8, 2, 2, 4)
AXES = ("grp", "zlo", "core", "zhi", "x")

SMEM = pl.BlockSpec(memory_space=pltpu.SMEM)
VMEM = pl.BlockSpec(memory_space=pltpu.VMEM)
HBM = pl.BlockSpec(memory_space=pl.ANY)


def call(kernel, ins, out, scratch=(), limit=16, flops=0):
    moved = sum(o.size * o.dtype.itemsize for o in out)
    many = len(out) > 1
    return pl.pallas_call(
        kernel,
        out_shape=tuple(out) if many else out[0],
        in_specs=ins,
        out_specs=tuple(VMEM for _ in out) if many else VMEM,
        scratch_shapes=list(scratch),
        compiler_params=pltpu.CompilerParams(vmem_limit_bytes=limit * 2**20),
        cost_estimate=pl.CostEstimate(flops=flops, bytes_accessed=2 * moved, transcendentals=0),
    )


def shape(dims, dtype):
    return jax.ShapeDtypeStruct(dims, dtype)


def pack_prompt(x_ref, rows_ref, out_ref):
    x = x_ref[0]
    rows = rows_ref[...].astype(f32)
    lat = rows[:, 0:128]
    rope = rows[0:16, LAT:WIDTH]
    for q in range(1, 4):
        lat = jnp.where(x == q, rows[:, 128 * q : 128 * q + 128], lat)
        if q < 3:
            rope = jnp.where(x == q, rows[16 * q : 16 * q + 16, LAT:WIDTH], rope)
    rope = jnp.concatenate([rope[0:8], rope[8:16]], 1)
    block = jnp.concatenate([lat, rope], 0).astype(bf16)
    for z in range(out_ref.shape[0]):
        out_ref[z] = block


def pack_block(lat, rope, q):
    lat = lat[:, 128 * q : 128 * q + 128].reshape(8, BLOCK, 128)
    if q < 3:
        rope = rope.reshape(8, BLOCK, ROPE)[:, 16 * q : 16 * q + 16]
        rope = jnp.concatenate([rope[:, 0:8], rope[:, 8:16]], 2)
    else:
        rope = jnp.zeros((8, 8, 128), f32)
    return jnp.concatenate([lat, rope], 1)


def bring_near(far_ref, near_ref, sem):
    copy = pltpu.make_async_copy(far_ref, near_ref, sem)
    copy.start()
    copy.wait()


NT = (((1,), (1,)), ((), ()))


def main_kernel(core_ref, len_ref, prompt_ref, resp_ref, q_ref, d_ref, k_ref, ds_ref, send_ref, keep_ref,
                keep_resp_ref, p_ref):
    core = core_ref[0]
    length = len_ref[0]
    for half in range(2):
        who = core if half == 0 else 1 - core
        at = 384 * half
        rope = []
        for q in range(4):
            got = prompt_ref[who, q]
            k_ref[at : at + 384, 128 * q : 128 * q + 128] = got[:, 0:48].reshape(384, 128)
            if q < 3:
                two = got[:, 48:56].astype(f32)
                rope += [two[:, :, 0:64], two[:, :, 64:128]]
        k_ref[at : at + 384, LAT:WIDTH] = jnp.concatenate(rope, 1).reshape(384, ROPE).astype(bf16)
    k_ref[768:896, :] = resp_ref[...]

    key_at = lax.broadcasted_iota(jnp.int32, (RESP, 256), 0)
    slot = lax.broadcasted_iota(jnp.int32, (RESP, 256), 1) % 128
    allowed = key_at <= slot
    live = lax.broadcasted_iota(jnp.int32, (1, 256), 1) % 128 < length
    for pair in range(4):
        q_pair = jnp.concatenate([q_ref[2 * pair], q_ref[2 * pair + 1]], 1)
        scores = jnp.dot(k_ref[...], q_pair, preferred_element_type=f32) * (softmax_scale * log2_e)
        scores = jnp.concatenate([scores[0:768], jnp.where(allowed, scores[768:896], masked_value)], 0)
        top = jnp.max(scores, axis=0, keepdims=True)
        expo = jnp.exp2(scores - top)
        total = jnp.sum(expo, axis=0, keepdims=True)
        d_pair = d_ref[256 * pair : 256 * pair + 256]
        d_prob = lax.dot_general(k_ref[:, 0:LAT], d_pair, NT, preferred_element_type=f32)
        inverse = 1.0 / total
        delta = jnp.sum(expo * d_prob, axis=0, keepdims=True) * inverse
        probs = expo * jnp.where(live, inverse, 0.0)
        p_ref[:, 256 * pair : 256 * pair + 256] = probs.astype(bf16)
        ds_ref[:, 256 * pair : 256 * pair + 256] = (probs * (d_prob - delta) * softmax_scale).astype(bf16)

    def grads(lo, hi):
        d_lat = jnp.dot(p_ref[lo:hi], d_ref[...], preferred_element_type=f32)
        q_all = jnp.concatenate([q_ref[h] for h in range(8)], 1)
        d_lat = d_lat + lax.dot_general(ds_ref[lo:hi], q_all[0:LAT], NT, preferred_element_type=f32)
        d_rope = lax.dot_general(ds_ref[lo:hi], q_all[LAT:WIDTH], NT, preferred_element_type=f32)
        return d_lat, d_rope

    lat, rope = grads(384, 768)
    for q in range(4):
        send_ref[q] = pack_block(lat, rope, q).astype(bf16)
    lat, rope = grads(0, 384)
    for q in range(4):
        keep_ref[q] = pack_block(lat, rope, q)
    lat, rope = grads(768, 896)
    for q in range(4):
        two = rope[32 * q : 32 * q + 32]
        two = jnp.concatenate([two[0:16], two[16:32]], 1)
        keep_resp_ref[q] = jnp.concatenate([lat[:, 128 * q : 128 * q + 128], two], 0).astype(bf16)


def query_kernel(k_ref, ds_ref, out_ref):
    k_t = k_ref[...].T
    for pair in range(4):
        got = jnp.dot(k_t, ds_ref[:, 256 * pair : 256 * pair + 256], preferred_element_type=f32).astype(bf16)
        out_ref[2 * pair] = got[:, 0:128]
        out_ref[2 * pair + 1] = got[:, 128:256]


def core_sum(core_ref, got_ref, keep_ref, keep_resp_ref, out_ref):
    other = 1 - core_ref[0]
    for q in range(4):
        both = keep_ref[q] + got_ref[other, q].astype(f32)
        out_ref[q, 0:448] = both.reshape(448, 128).astype(bf16)
        out_ref[q, 448:592] = keep_resp_ref[q]


def x_sum(got_ref, prompt_ref, resp_ref):
    total = got_ref[0].astype(f32)
    for q in range(1, 4):
        total = total + got_ref[q].astype(f32)
    total = total.astype(bf16)
    for z in range(8):
        block = total[PACKED * z : PACKED * z + PACKED]
        prompt_ref[2 * z] = block
        prompt_ref[2 * z + 1] = block
    resp_ref[...] = total[448:592]


def last_sum(got_ref, mine_ref, far_ref, out_ref):
    total = got_ref[0].astype(f32)
    for z in range(1, 16):
        total = total + got_ref[z].astype(f32)
    resp = (mine_ref[...].astype(f32) + far_ref[...].astype(f32)).astype(bf16)
    total = total.astype(bf16)
    for q in range(4):
        out_ref[q, 0:RESP_PACKED] = resp
        out_ref[q, RESP_PACKED : RESP_PACKED + PACKED] = total


def unpack(got_ref, prompt_ref, resp_ref):
    resp_rope, prompt_rope = [], []
    for q in range(4):
        got = got_ref[q].astype(f32)
        resp_ref[128 * q : 128 * q + 128, :] = got[0:128].T.astype(bf16)
        resp_rope += [got[128:144, 0:64], got[128:144, 64:128]]
        prompt_ref[:, 128 * q : 128 * q + 128] = got[144:192].astype(bf16)
        if q < 3:
            prompt_rope += [got[192:200, 0:64], got[192:200, 64:128]]
    resp_ref[LAT:WIDTH, :] = jnp.concatenate(resp_rope, 0).T.astype(bf16)
    prompt_ref[:, LAT:WIDTH] = jnp.concatenate(prompt_rope, 0).astype(bf16)


def body(queries, grad_out, prompt_kv, resp_kv, lengths):
    x_at = lax.axis_index("x").astype(jnp.int32).reshape(1)
    core_at = lax.axis_index("core").astype(jnp.int32).reshape(1)
    q_t = jnp.transpose(queries, (1, 2, 0))
    d_heads = jnp.transpose(grad_out, (1, 0, 2)).reshape(8 * RESP, LAT)

    q_t = call(bring_near, [HBM], [shape((8, WIDTH, 128), bf16)], scratch=[pltpu.SemaphoreType.DMA])(q_t)
    mine = call(pack_prompt, [SMEM, VMEM], [shape((8, PACKED, 128), bf16)])(x_at, prompt_kv)
    along_z = lax.all_to_all(mine, "zlo", 0, 0, tiled=True)
    along_x = jnp.broadcast_to(along_z[None], (4, 8, PACKED, 128))
    along_x = lax.all_to_all(along_x, "x", 0, 0, tiled=True)
    prompt = lax.all_gather(along_x, "core")

    keys, d_score, send, keep, keep_resp = call(
        main_kernel,
        [SMEM, SMEM, VMEM, VMEM, VMEM, VMEM],
        [
            shape((896, WIDTH), bf16),
            shape((896, 1024), bf16),
            shape((4, 8, PACKED, 128), bf16),
            shape((4, 8, PACKED, 128), f32),
            shape((4, RESP_PACKED, 128), bf16),
        ],
        scratch=[pltpu.VMEM((896, 1024), bf16)],
        limit=40,
        flops=4 * 2 * 1024 * 896 * 576,
    )(core_at, lengths, prompt, resp_kv, q_t, d_heads)

    got = lax.all_gather(send, "core")
    parts = call(core_sum, [SMEM, VMEM, VMEM, VMEM], [shape((4, 592, 128), bf16)])(core_at, got, keep, keep_resp)
    parts = lax.all_to_all(parts, "x", 0, 0, tiled=True)
    d_query = call(
        query_kernel, [VMEM, VMEM], [shape((8, WIDTH, 128), bf16)], limit=24, flops=2 * 1024 * 896 * 576
    )(keys, d_score)
    terms, resp_mine = call(x_sum, [VMEM], [shape((16, PACKED, 128), bf16), shape((RESP_PACKED, 128), bf16)])(parts)
    terms = lax.all_to_all(terms, ("zlo", "zhi"), 0, 0, tiled=True)
    resp_far = lax.ppermute(resp_mine, "zhi", [(0, 1), (1, 0)])
    final = call(last_sum, [VMEM, VMEM, VMEM], [shape((4, 200, 128), bf16)])(terms, resp_mine, resp_far)
    final = lax.all_to_all(final, "x", 0, 0, tiled=True)
    grad_prompt, grad_resp = call(unpack, [VMEM], [shape((BLOCK, WIDTH), bf16), shape((WIDTH, RESP), bf16)])(final)
    return (jnp.transpose(d_query, (2, 0, 1)), grad_prompt, grad_resp.T)


def solution(mesh):
    split = Mesh(mesh.devices.reshape(GRID), AXES)
    rows = ("grp", "zlo", "core")
    heads = ("zhi", "x")
    return jax.shard_map(
        body,
        mesh=split,
        in_specs=(P(rows, heads, None), P(rows, heads, None), P(rows, None), P(rows, None), P(rows)),
        out_specs=(P(rows, heads, None), P(rows, None), P(rows, None)),
        check_vma=False,
    )
```

```python
import functools

import jax
import jax.numpy as jnp
from jax import lax
from jax.experimental import pallas as pl
from jax.experimental.pallas import tpu as pltpu
from jax.sharding import Mesh, PartitionSpec as P

softmax_scale = 192 ** (-0.5)
log2_e = 1.4426950408889634
masked_value = -1e30
f32, bf16 = jnp.float32, jnp.bfloat16

LAT, ROPE, WIDTH = 512, 64, 576
BLOCK, PACKED = 48, 56
RESP, RESP_PACKED = 128, 144
GRID = (4, 8, 2, 2, 4)
AXES = ("grp", "zlo", "core", "zhi", "x")

SMEM = pl.BlockSpec(memory_space=pltpu.SMEM)
VMEM = pl.BlockSpec(memory_space=pltpu.VMEM)
HBM = pl.BlockSpec(memory_space=pl.ANY)


SCR = [pltpu.VMEM((896, 1024), bf16), pltpu.VMEM((2, 896, 256), f32), pltpu.VMEM((2, 896, 256), f32)]


def call(kernel, ins, out, scratch=(), limit=16, flops=0):
    moved = sum(o.size * o.dtype.itemsize for o in out)
    many = len(out) > 1
    return pl.pallas_call(
        kernel,
        out_shape=tuple(out) if many else out[0],
        in_specs=ins,
        out_specs=tuple(VMEM for _ in out) if many else VMEM,
        scratch_shapes=list(scratch),
        compiler_params=pltpu.CompilerParams(vmem_limit_bytes=limit * 2**20),
        cost_estimate=pl.CostEstimate(flops=flops, bytes_accessed=2 * moved, transcendentals=0),
    )


def shape(dims, dtype):
    return jax.ShapeDtypeStruct(dims, dtype)


def pack_prompt(x_ref, rows_ref, out_ref):
    x = x_ref[0]
    rows = rows_ref[...].astype(f32)
    lat = rows[:, 0:128]
    rope = rows[0:16, LAT:WIDTH]
    for q in range(1, 4):
        lat = jnp.where(x == q, rows[:, 128 * q : 128 * q + 128], lat)
        if q < 3:
            rope = jnp.where(x == q, rows[16 * q : 16 * q + 16, LAT:WIDTH], rope)
    rope = jnp.concatenate([rope[0:8], rope[8:16]], 1)
    block = jnp.concatenate([lat, rope], 0).astype(bf16)
    for z in range(out_ref.shape[0]):
        out_ref[z] = block


def pack_block(lat, rope, q):
    lat = lat[:, 128 * q : 128 * q + 128].reshape(8, BLOCK, 128)
    if q < 3:
        rope = rope.reshape(8, BLOCK, ROPE)[:, 16 * q : 16 * q + 16]
        rope = jnp.concatenate([rope[:, 0:8], rope[:, 8:16]], 2)
    else:
        rope = jnp.zeros((8, 8, 128), f32)
    return jnp.concatenate([lat, rope], 1)


def bring_near(far_ref, near_ref, sem):
    copy = pltpu.make_async_copy(far_ref, near_ref, sem)
    copy.start()
    copy.wait()


NT = (((1,), (1,)), ((), ()))


def main_kernel(core_ref, len_ref, prompt_ref, resp_ref, q_ref, d_ref, k_ref, ds_ref, send_ref, keep_ref,
                keep_resp_ref, p_ref, s_ref, dp_ref):
    core = core_ref[0]
    length = len_ref[0]
    for half in range(2):
        who = core if half == 0 else 1 - core
        at = 384 * half
        rope = []
        for q in range(4):
            got = prompt_ref[who, q]
            k_ref[at : at + 384, 128 * q : 128 * q + 128] = got[:, 0:48].reshape(384, 128)
            if q < 3:
                two = got[:, 48:56].astype(f32)
                rope += [two[:, :, 0:64], two[:, :, 64:128]]
        k_ref[at : at + 384, LAT:WIDTH] = jnp.concatenate(rope, 1).reshape(384, ROPE).astype(bf16)
    k_ref[768:896, :] = resp_ref[...]

    key_at = lax.broadcasted_iota(jnp.int32, (RESP, 256), 0)
    slot = lax.broadcasted_iota(jnp.int32, (RESP, 256), 1) % 128
    allowed = key_at <= slot
    live = lax.broadcasted_iota(jnp.int32, (1, 256), 1) % 128 < length
    def products(pair):
        q_pair = jnp.concatenate([q_ref[2 * pair], q_ref[2 * pair + 1]], 1)
        scores = jnp.dot(k_ref[...], q_pair, preferred_element_type=f32)
        d_pair = d_ref[256 * pair : 256 * pair + 256]
        d_prob = lax.dot_general(k_ref[:, 0:LAT], d_pair, NT, preferred_element_type=f32)
        s_ref[pair % 2] = scores
        dp_ref[pair % 2] = d_prob

    def weights(pair):
        at = pair % 2
        tops = [s_ref[at, 128 * i : 128 * i + 128].reshape(16, 8, 256).max(0) for i in range(6)]
        last = jnp.where(allowed, s_ref[at, 768:896], masked_value)
        s_ref[at, 768:896] = last
        tops.append(last.reshape(16, 8, 256).max(0))
        top = functools.reduce(jnp.maximum, tops).max(0, keepdims=True)
        total = jnp.zeros((8, 256), f32)
        weighed = jnp.zeros((8, 256), f32)
        for i in range(7):
            rows = slice(128 * i, 128 * i + 128)
            expo = jnp.exp2((s_ref[at, rows] - top) * (softmax_scale * log2_e))
            s_ref[at, rows] = expo
            total = total + expo.reshape(16, 8, 256).sum(0)
            weighed = weighed + (expo * dp_ref[at, rows]).reshape(16, 8, 256).sum(0)
        inverse = 1.0 / total.sum(0, keepdims=True)
        delta = weighed.sum(0, keepdims=True) * inverse
        share = jnp.where(live, inverse, 0.0)
        scaled = share * softmax_scale
        for i in range(7):
            rows = slice(128 * i, 128 * i + 128)
            expo = s_ref[at, rows]
            p_ref[rows, 256 * pair : 256 * pair + 256] = (expo * share).astype(bf16)
            ds_ref[rows, 256 * pair : 256 * pair + 256] = (expo * scaled * (dp_ref[at, rows] - delta)).astype(bf16)

    products(0)
    for pair in range(4):
        if pair < 3:
            products(pair + 1)
        weights(pair)

    def grads(lo, hi):
        d_lat = jnp.dot(p_ref[lo:hi], d_ref[...], preferred_element_type=f32)
        q_all = jnp.concatenate([q_ref[h] for h in range(8)], 1)
        d_lat = d_lat + lax.dot_general(ds_ref[lo:hi], q_all[0:LAT], NT, preferred_element_type=f32)
        d_rope = lax.dot_general(ds_ref[lo:hi], q_all[LAT:WIDTH], NT, preferred_element_type=f32)
        return d_lat, d_rope

    lat, rope = grads(384, 768)
    for q in range(4):
        send_ref[q] = pack_block(lat, rope, q).astype(bf16)
    lat, rope = grads(0, 384)
    for q in range(4):
        keep_ref[q] = pack_block(lat, rope, q)
    lat, rope = grads(768, 896)
    for q in range(4):
        two = rope[32 * q : 32 * q + 32]
        two = jnp.concatenate([two[0:16], two[16:32]], 1)
        keep_resp_ref[q] = jnp.concatenate([lat[:, 128 * q : 128 * q + 128], two], 0).astype(bf16)


def query_kernel(k_ref, ds_ref, out_ref):
    k_t = k_ref[...].T
    for pair in range(4):
        got = jnp.dot(k_t, ds_ref[:, 256 * pair : 256 * pair + 256], preferred_element_type=f32).astype(bf16)
        out_ref[2 * pair] = got[:, 0:128]
        out_ref[2 * pair + 1] = got[:, 128:256]


def core_sum(core_ref, got_ref, keep_ref, keep_resp_ref, out_ref):
    other = 1 - core_ref[0]
    for q in range(4):
        both = keep_ref[q] + got_ref[other, q].astype(f32)
        out_ref[q, 0:448] = both.reshape(448, 128).astype(bf16)
        out_ref[q, 448:592] = keep_resp_ref[q]


def x_sum(got_ref, prompt_ref, resp_ref):
    total = got_ref[0].astype(f32)
    for q in range(1, 4):
        total = total + got_ref[q].astype(f32)
    total = total.astype(bf16)
    for z in range(8):
        block = total[PACKED * z : PACKED * z + PACKED]
        prompt_ref[z] = block
        prompt_ref[z + 8] = block
    resp_ref[...] = total[448:592]


def last_sum(got_ref, mine_ref, far_ref, out_ref):
    total = got_ref[0].astype(f32)
    for z in range(1, 16):
        total = total + got_ref[z].astype(f32)
    resp = (mine_ref[...].astype(f32) + far_ref[...].astype(f32)).astype(bf16)
    total = total.astype(bf16)
    for q in range(4):
        out_ref[q, 0:RESP_PACKED] = resp
        out_ref[q, RESP_PACKED : RESP_PACKED + PACKED] = total


def unpack(got_ref, prompt_ref, resp_ref):
    resp_rope, prompt_rope = [], []
    for q in range(4):
        got = got_ref[q].astype(f32)
        resp_ref[128 * q : 128 * q + 128, :] = got_ref[q, 0:128].T
        resp_rope += [got[128:144, 0:64], got[128:144, 64:128]]
        prompt_ref[:, 128 * q : 128 * q + 128] = got[144:192].astype(bf16)
        if q < 3:
            prompt_rope += [got[192:200, 0:64], got[192:200, 64:128]]
    resp_ref[LAT:WIDTH, :] = jnp.concatenate(resp_rope, 0).T.astype(bf16)
    prompt_ref[:, LAT:WIDTH] = jnp.concatenate(prompt_rope, 0).astype(bf16)


def body(queries, grad_out, prompt_kv, resp_kv, lengths):
    x_at = lax.axis_index("x").astype(jnp.int32).reshape(1)
    core_at = lax.axis_index("core").astype(jnp.int32).reshape(1)
    q_t = jnp.transpose(queries, (1, 2, 0))
    d_heads = jnp.transpose(grad_out, (1, 0, 2)).reshape(8 * RESP, LAT)

    q_t = call(bring_near, [HBM], [shape((8, WIDTH, 128), bf16)], scratch=[pltpu.SemaphoreType.DMA])(q_t)
    mine = call(pack_prompt, [SMEM, VMEM], [shape((8, PACKED, 128), bf16)])(x_at, prompt_kv)
    along_z = lax.all_to_all(mine, "zlo", 0, 0, tiled=True)
    along_x = jnp.broadcast_to(along_z[None], (4, 8, PACKED, 128))
    along_x = lax.all_to_all(along_x, "x", 0, 0, tiled=True)
    prompt = lax.all_gather(along_x, "core")

    keys, d_score, send, keep, keep_resp = call(
        main_kernel,
        [SMEM, SMEM, VMEM, VMEM, VMEM, VMEM],
        [
            shape((896, WIDTH), bf16),
            shape((896, 1024), bf16),
            shape((4, 8, PACKED, 128), bf16),
            shape((4, 8, PACKED, 128), f32),
            shape((4, RESP_PACKED, 128), bf16),
        ],
        scratch=SCR,
        limit=40,
        flops=4 * 2 * 1024 * 896 * 576,
    )(core_at, lengths, prompt, resp_kv, q_t, d_heads)

    got = lax.all_gather(send, "core")
    parts = call(core_sum, [SMEM, VMEM, VMEM, VMEM], [shape((4, 592, 128), bf16)])(core_at, got, keep, keep_resp)
    parts = lax.all_to_all(parts, "x", 0, 0, tiled=True)
    d_query = call(
        query_kernel, [VMEM, VMEM], [shape((8, WIDTH, 128), bf16)], limit=24, flops=2 * 1024 * 896 * 576
    )(keys, d_score)
    terms, resp_mine = call(x_sum, [VMEM], [shape((16, PACKED, 128), bf16), shape((RESP_PACKED, 128), bf16)])(parts)
    terms = lax.all_to_all(terms, ("zhi", "zlo"), 0, 0, tiled=True)
    resp_far = lax.ppermute(resp_mine, "zhi", [(0, 1), (1, 0)])
    resp_far, d_query = lax.optimization_barrier((resp_far, d_query))
    final = call(last_sum, [VMEM, VMEM, VMEM], [shape((4, 200, 128), bf16)])(terms, resp_mine, resp_far)
    final = lax.all_to_all(final, "x", 0, 0, tiled=True)
    grad_prompt, grad_resp = call(unpack, [VMEM], [shape((BLOCK, WIDTH), bf16), shape((WIDTH, RESP), bf16)])(final)
    return (jnp.transpose(d_query, (2, 0, 1)), grad_prompt, grad_resp.T)


def solution(mesh):
    split = Mesh(mesh.devices.reshape(GRID), AXES)
    rows = ("grp", "zlo", "core")
    heads = ("zhi", "x")
    return jax.shard_map(
        body,
        mesh=split,
        in_specs=(P(rows, heads, None), P(rows, heads, None), P(rows, None), P(rows, None), P(rows)),
        out_specs=(P(rows, heads, None), P(rows, None), P(rows, None)),
        check_vma=False,
    )
```
